32 devices in a mesh: face: 2 (over core), sub: 16 (over z, y, x).
Axes of the slice: x: 2, y: 2, z: 4, core: 2. Of those that a mesh axis runs over, the one named last changes fastest.
Arguments:
- features: bfloat16 [768, 24, 192], P(('face', 'sub')), may hold values from -6 to 6
- w_first: bfloat16 [3, 3, 192, 192], replicated, may hold values from -0.15625 to 0.15625
- b_first: float32 [192], replicated, may hold values from -3 to 3
- w_second: bfloat16 [3, 3, 192, 192], replicated, may hold values from -0.15625 to 0.15625
- neighbours: int32 [32, 4], replicated, may hold values from 0 to 31, as said below
- rotations: int32 [32, 4], replicated, may hold values from 0 to 3
- cotangent: bfloat16 [384, 12, 192], P(('face', 'sub')), may hold values from -6 to 6
Outputs:
- pooled: bfloat16 [384, 12, 192], P(('face', 'sub'))
- grad_input: bfloat16 [768, 24, 192], P(('face', 'sub'))
- grad_w1: float32 [3, 3, 192, 192], replicated
- grad_b1: float32 [192], replicated
- grad_w2: float32 [3, 3, 192, 192], replicated
The draws below stay inside these ranges and needn't reach their ends.
Inputs may be any that keep to these rules, and one draw needn't show every extreme that they name: neighbours[d, e] is a tile f * 16 + s other than d; it has the same f as d or the same s as d; two tiles of the same f share at most one edge, and no tile names the same tile of its own f at two edges.
All inputs are finite; a program needn't handle non-finite values.
Results may differ from the reference program's by a relative error of at most 0.012.
Values may be sent and summed in bfloat16 or wider, within the bound.
A program may use at most 64 MiB of HBM per device.

```python
import math
import jax
import jax.numpy as jnp
import numpy as np
from jax import lax

C = 192
TB = 24
HALF = 12
DEVS = 32
ROWS = 768
HALF_ROWS = 384
N_FACE = 2
N_SUB = 16


def draw_neighbours(key, part):
    bit_count = N_SUB.bit_length() - 1
    places = []
    for sub_pos in range(N_SUB):
        column = 0
        row_pos = 0
        for bit_pos in range(bit_count):
            if bit_pos % 2 == 0:
                column = column + ((sub_pos >> bit_pos & 1) << bit_pos // 2)
            else:
                row_pos = row_pos + ((sub_pos >> bit_pos & 1) << bit_pos // 2)
        places.append((row_pos, column))
    finder = {}
    for sub_pos in range(N_SUB):
        finder[places[sub_pos]] = sub_pos
    step_list = [(-1, 0), (0, 1), (1, 0), (0, -1)]
    inside_sub = np.zeros((N_SUB, 4), np.int32)
    inside_flag = np.zeros((N_SUB, 4), np.int32)
    for sub_pos in range(N_SUB):
        for border in range(4):
            target = (places[sub_pos][0] + step_list[border][0], places[sub_pos][1] + step_list[border][1])
            if target in finder:
                inside_sub[sub_pos, border] = finder[target]
                inside_flag[sub_pos, border] = 1
            else:
                inside_sub[sub_pos, border] = sub_pos
    positions = jnp.arange(N_SUB, dtype=jnp.int32)
    shuffled = jax.random.permutation(jax.random.fold_in(key, 13), N_SUB).astype(jnp.int32)
    wanted = (shuffled[0] + N_SUB // 2) % N_SUB
    where_wanted = jnp.sum(jnp.where(shuffled == wanted, positions, 0)).astype(jnp.int32)
    second_label = shuffled[1]
    labels = jnp.where(positions == 1, wanted, jnp.where(positions == where_wanted, second_label, shuffled)).astype(jnp.int32)
    inside_label = labels[jnp.asarray(inside_sub)]
    face_order = jax.random.permutation(jax.random.fold_in(key, 11), N_FACE).astype(jnp.int32)
    inverse = jnp.argsort(face_order).astype(jnp.int32)
    shifts = jax.random.randint(jax.random.fold_in(key, 12), (4,), 1, N_FACE).astype(jnp.int32)
    partner = inverse[(face_order[:, None] + shifts[None, :]) % N_FACE]
    face_ids = jnp.arange(N_FACE, dtype=jnp.int32)
    owner_face = jnp.where(jnp.asarray(inside_flag)[None] == 1, face_ids[:, None, None], partner[:, None, :])
    by_position = owner_face * N_SUB + inside_label[None]
    result = jnp.zeros((N_FACE, N_SUB, 4), jnp.int32).at[:, labels].set(by_position)
    return result.reshape(N_FACE * N_SUB, 4).astype(jnp.int32)


def with_ends(entries, own_key, least, largest):
    index_at = [jax.random.randint(jax.random.fold_in(own_key, axis), (), 0, length) for axis, length in enumerate(entries.shape)]
    widest = entries.shape.index(max(entries.shape))
    next_to = index_at[:widest] + [(index_at[widest] + 1) % entries.shape[widest]] + index_at[widest + 1:]
    return entries.at[tuple(index_at)].set(least).at[tuple(next_to)].set(largest)


def block_levels(key, shape, cuts, least, high):
    level = 1.0
    for position, blocks in cuts:
        steps = jax.random.uniform(jax.random.fold_in(jax.random.fold_in(key, 6), position), (blocks,), jnp.float32, least / len(cuts), high / len(cuts))
        level = level * jnp.repeat(jnp.exp(steps), shape[position] // blocks).reshape((-1,) + (1,) * (len(shape) - 1 - position))
    return level


def gaussian(rng, shape, deviation, limit, pieces=(), held_as=jnp.bfloat16):
    values = jax.random.normal(rng, shape, jnp.float32) * deviation
    if len(pieces) > 0:
        values = block_levels(rng, shape, pieces, -0.22, 0.18) * values
    return jnp.clip(values, min=-limit, max=limit).astype(held_as)


def setup_inputs(seed: int = 0) -> dict:
    arg_keys = jax.random.split(jax.random.key(seed), 8)
    return {
        "features": gaussian(arg_keys[0], (ROWS, TB, C), 1.0, 6.0, ((0, 32),)),
        "w_first": gaussian(arg_keys[1], (3, 3, C, C), (9 * C) ** -0.5, 0.15625),
        "b_first": gaussian(arg_keys[2], (C,), 0.5, 3.0, (), jnp.float32),
        "w_second": gaussian(arg_keys[3], (3, 3, C, C), (9 * C) ** -0.5, 0.15625),
        "neighbours": draw_neighbours(jax.random.fold_in(arg_keys[7], 71), 0),
        "rotations": with_ends(jax.random.randint(arg_keys[5], (DEVS, 4), 0, 4), jax.random.fold_in(arg_keys[5], 1), 0, 3).astype(jnp.int32),
        "cotangent": gaussian(arg_keys[6], (HALF_ROWS, HALF, C), 1.0, 6.0, ((0, 32),)),
    }


def rim_lookup():
    return np.array([[[0, 0], [1, 0], [2, 0], [3, 0]], [[1, 0], [2, 1], [3, 0], [0, 1]], [[2, 1], [3, 1], [0, 1], [1, 1]], [[3, 1], [0, 0], [1, 1], [2, 0]]], np.int32)

def rim_codes(rotations):
    lookup = rim_lookup()[:, [2, 3, 0, 1], :]
    anchor_tab = jnp.asarray(lookup[:, :, 0])
    flip_tab = jnp.asarray(lookup[:, :, 1])
    border_ids = jnp.arange(4, dtype=jnp.int32)
    anchors = anchor_tab[rotations, border_ids[None, :]]
    flip_codes = flip_tab[rotations, border_ids[None, :]]
    return (anchors, flip_codes)

def pad_tiles(tile_set, neighbours, rotations):
    anchors, flip_codes = rim_codes(rotations)
    edge_rows = jnp.stack([tile_set[:, 0], tile_set[:, :, -1], tile_set[:, -1], tile_set[:, :, 0]], axis=1)
    picked = edge_rows[neighbours, anchors]
    picked = jnp.where(flip_codes[:, :, None, None] == 1, picked[:, :, ::-1], picked)
    padded = jnp.pad(tile_set, ((0, 0), (1, 1), (1, 1), (0, 0)))
    padded = padded.at[:, 0, 1:-1].set(picked[:, 0])
    padded = padded.at[:, 1:-1, -1].set(picked[:, 1])
    padded = padded.at[:, -1, 1:-1].set(picked[:, 2])
    padded = padded.at[:, 1:-1, 0].set(picked[:, 3])
    return padded

def correlate(padded, weights):
    extent = padded.shape[1] - 2
    summed = jnp.zeros((padded.shape[0], extent, extent, weights.shape[3]), jnp.float32)
    for row_off in range(3):
        for col_off in range(3):
            window = padded[:, row_off:row_off + extent, col_off:col_off + extent]
            summed = summed + jnp.einsum('dijc,co->dijo', window, weights[row_off, col_off].astype(jnp.float32))
    return summed

def spread_back(grads, weights):
    extent = grads.shape[1]
    summed = jnp.zeros((grads.shape[0], extent + 2, extent + 2, weights.shape[2]), jnp.float32)
    for row_off in range(3):
        for col_off in range(3):
            portion = jnp.einsum('dijo,co->dijc', grads, weights[row_off, col_off].astype(jnp.float32))
            summed = summed.at[:, row_off:row_off + extent, col_off:col_off + extent].add(portion)
    return summed

def weight_grad(padded, grads):
    extent = grads.shape[1]
    blocks_out = []
    for row_off in range(3):
        for col_off in range(3):
            window = padded[:, row_off:row_off + extent, col_off:col_off + extent]
            blocks_out.append(jnp.einsum('dijc,dijo->co', window, grads))
    return jnp.stack(blocks_out, axis=0).reshape(3, 3, padded.shape[3], grads.shape[3])

def fold_back(summed, neighbours, rotations):
    anchors, flip_codes = rim_codes(rotations)
    middle = summed[:, 1:-1, 1:-1]
    outer = jnp.stack([summed[:, 0, 1:-1], summed[:, 1:-1, -1], summed[:, -1, 1:-1], summed[:, 1:-1, 0]], axis=1)
    outer = jnp.where(flip_codes[:, :, None, None] == 1, outer[:, :, ::-1], outer)
    arrived = jnp.zeros_like(outer).at[neighbours, anchors].add(outer)
    middle = middle.at[:, 0].add(arrived[:, 0])
    middle = middle.at[:, :, -1].add(arrived[:, 1])
    middle = middle.at[:, -1].add(arrived[:, 2])
    middle = middle.at[:, :, 0].add(arrived[:, 3])
    return middle

def reference(features, w_first, b_first, w_second, neighbours, rotations, cotangent):
    tile_set = features.reshape(DEVS, TB, TB, C).astype(jnp.float32)
    padded_in = pad_tiles(tile_set, neighbours, rotations)
    hidden = correlate(padded_in, w_first) + b_first
    active = lax.optimization_barrier(jax.nn.silu(hidden).astype(jnp.bfloat16)).astype(jnp.float32)
    padded_act = pad_tiles(active, neighbours, rotations)
    second = correlate(padded_act, w_second)
    summed_out = tile_set + second
    pooled = summed_out.reshape(DEVS, HALF, 2, HALF, 2, C).mean(axis=(2, 4)).astype(jnp.bfloat16)
    upward = cotangent.reshape(DEVS, HALF, HALF, C).astype(jnp.float32) * 0.25
    grad_out = jnp.broadcast_to(upward[:, :, None, :, None, :], (DEVS, HALF, 2, HALF, 2, C)).reshape(DEVS, TB, TB, C)
    sum_w2 = weight_grad(padded_act, grad_out)
    grad_active = fold_back(spread_back(grad_out, w_second), neighbours, rotations)
    grad_active = lax.optimization_barrier(grad_active.astype(jnp.bfloat16)).astype(jnp.float32)
    sigmoid_h = jax.nn.sigmoid(hidden)
    grad_hidden = grad_active * sigmoid_h * (1.0 + hidden * (1.0 - sigmoid_h))
    grad_hidden = lax.optimization_barrier(grad_hidden.astype(jnp.bfloat16)).astype(jnp.float32)
    sum_b1 = lax.optimization_barrier(jnp.sum(grad_hidden, axis=(0, 1, 2)))
    sum_w1 = weight_grad(padded_in, grad_hidden)
    grad_input = fold_back(spread_back(grad_hidden, w_first), neighbours, rotations) + grad_out
    grad_scale = 1.0 / math.sqrt(DEVS * TB * TB)
    return (pooled.reshape(DEVS * HALF, HALF, C), grad_input.astype(jnp.bfloat16).reshape(DEVS * TB, TB, C), sum_w1 * grad_scale, sum_b1 * grad_scale, sum_w2 * grad_scale)
```

```python
import functools
import math

import jax
import jax.numpy as jnp
from jax import lax
from jax.experimental import pallas as pl
from jax.experimental.pallas import tpu as pltpu
from jax.sharding import PartitionSpec as P

W = 32
F32, BF16 = jnp.float32, jnp.bfloat16
MESH = pl.DeviceIdType.MESH


def iota(shape, dim):
    return lax.broadcasted_iota(jnp.int32, shape, dim)


def hot(mask):
    return jnp.where(mask, 1.0, 0.0).astype(BF16)


def dot(a, b, ca=1, cb=0):
    return lax.dot_general(a, b, (((ca,), (cb,)), ((), ())), preferred_element_type=F32)


def split(x):
    hi = x.astype(BF16)
    return hi, (x - hi.astype(F32)).astype(BF16)


def rim_pos(q, extent, pad):
    e, p = q // W, q % W + pad
    far = extent - 1 + 2 * pad
    pos = jnp.where(e == 0, p, jnp.where(e == 1, p * W + far, jnp.where(e == 2, far * W + p, p * W)))
    return jnp.where(q % W < extent, pos, -1)


def kernel(S, F, chunk, scale, nbr, rot, feat, cot, w1, b1, w2,
           pooled, gin, gw1, gb1, gw2,
           send_mat, recv_mat, pad_in, pad_act, gpad1, gpad2, cotp,
           win_in, win_act, gs1, gs2, hidden, second, pg, gact,
           ex_out, ex_in, wf, wb, w1in, red, accf, w2in, gath,
           ex_ss, ex_rs, w_ss, w_rs):
    T, C = feat.shape[0], feat.shape[2]
    H = T // 2
    face, sub = lax.axis_index("face"), lax.axis_index("sub")
    me = face * S + sub
    part = chunk * S
    M, MP = T * W, (T + 2) * W

    def peers(count, mine, body):
        def step(d, c):
            body(lax.rem(mine + d, count))
            return c
        lax.fori_loop(1, count, step, 0)

    barrier = pltpu.get_barrier_semaphore()
    peers(S, sub, lambda j: pl.semaphore_signal(barrier, inc=1, device_id=(face, j), device_id_type=MESH))
    peers(F, face, lambda f: pl.semaphore_signal(barrier, inc=1, device_id=(f, sub), device_id_type=MESH))

    p32 = iota((W, 4 * W), 0)
    c32 = iota((W, 4 * W), 1)

    def put_slot(k, hit, src, flip, edge):
        tgt = jnp.where(flip == 1, src * W + T - 1 - p32, src * W + p32)
        base = pl.multiple_of(k * W, W)
        send_mat[pl.ds(base, W), :] = hot((c32 == tgt) & (p32 < T) & (hit == 1))
        recv_mat[pl.ds(base, W), :] = hot((c32 == edge * W + p32) & (p32 < T) & (edge >= 0))

    def edge_code(tile, e):
        r = rot[tile * 4 + e]
        x = (e + 2) % 4
        src = lax.rem(x + r, 4)
        odd = x % 2
        flip = jnp.where(r == 2, 1, jnp.where(r == 1, odd, jnp.where(r == 3, 1 - odd, 0)))
        return nbr[tile * 4 + e] == me, src, flip

    def in_face(j, c):
        hit, src, flip, edge = jnp.int32(0), jnp.int32(0), jnp.int32(0), jnp.int32(-1)
        for e in range(4):
            h, s, f = edge_code(face * S + j, e)
            hit = jnp.where(h, 1, hit)
            src = jnp.where(h, s, src)
            flip = jnp.where(h, f, flip)
            edge = jnp.where(nbr[me * 4 + e] == face * S + j, e, edge)
        put_slot(j, hit, src, flip, edge)
        return c

    lax.fori_loop(0, S, in_face, 0)

    def cross(f, c):
        for e in range(4):
            h, s, fl = edge_code(f * S + sub, e)
            other = f != face
            hit = jnp.where(h & other, 1, 0)
            edge = jnp.where((nbr[me * 4 + e] == f * S + sub) & other, e, -1)
            put_slot(S + f * 4 + e, hit, s, fl, edge)
        return c

    lax.fori_loop(0, F, cross, 0)

    for ph in range(4):
        ex_in[ph, pl.ds(pl.multiple_of(sub * W, W), W), :] = jnp.zeros((W, C), BF16)
        ex_in[ph, pl.ds(pl.multiple_of((S + 4 * face) * W, W), 4 * W), :] = jnp.zeros((4 * W, C), BF16)

    def ex_sub(ph, j, s_in, r_idx):
        return pltpu.make_async_remote_copy(
            src_ref=ex_out.at[ph, pl.ds(pl.multiple_of(j * W, W), W), :],
            dst_ref=ex_in.at[ph, pl.ds(pl.multiple_of(s_in * W, W), W), :],
            send_sem=ex_ss.at[ph, j], recv_sem=ex_rs.at[ph, r_idx],
            device_id=(face, j), device_id_type=MESH)

    def ex_face(ph, f, f_in):
        return pltpu.make_async_remote_copy(
            src_ref=ex_out.at[ph, pl.ds(pl.multiple_of((S + 4 * f) * W, W), 4 * W), :],
            dst_ref=ex_in.at[ph, pl.ds(pl.multiple_of((S + 4 * f_in) * W, W), 4 * W), :],
            send_sem=ex_ss.at[ph, S + f], recv_sem=ex_rs.at[ph, S + f_in],
            device_id=(f, sub), device_id_type=MESH)

    def ex_start(ph, mat, rims):
        ex_out[ph] = dot(mat[...], rims).astype(BF16)
        peers(S, sub, lambda j: ex_sub(ph, j, sub, sub).start())
        peers(F, face, lambda f: ex_face(ph, f, face).start())

    def ex_wait(ph, mat):
        peers(S, sub, lambda j: ex_sub(ph, j, j, j).wait_recv())
        peers(F, face, lambda f: ex_face(ph, f, f).wait_recv())
        return dot(mat[...], ex_in[ph], 0, 0)

    def ex_drain(ph):
        peers(S, sub, lambda j: ex_sub(ph, j, sub, sub).wait_send())
        peers(F, face, lambda f: ex_face(ph, f, face).wait_send())

    own_rims = hot(iota((4 * W, M), 1) == rim_pos(iota((4 * W, M), 0), T, 0))
    pad_rims = hot(iota((4 * W, MP), 1) == rim_pos(iota((4 * W, MP), 0), T, 1))
    own_place = hot(iota((M, 4 * W), 0) == rim_pos(iota((M, 4 * W), 1), T, 0))
    pad_place = hot(iota((MP, 4 * W), 0) == rim_pos(iota((MP, 4 * W), 1), T, 1))

    def windows(src, dst, rows):
        for b in range(3):
            dst[b] = src[:, b:b + W, :].reshape(rows * W, C).astype(BF16)

    def add_halo(padded, halo):
        placed = dot(pad_place, halo.astype(BF16)).reshape(T + 2, W, C)
        padded[:, 0:W, :] = padded[:, 0:W, :] + placed

    def conv(win, wt, out, rows, back):
        half = rows // 2

        def step(i, c):
            acc = None
            for a in range(3):
                for b in range(3):
                    off = pl.multiple_of(i * half, 16) + a * W
                    x = win[b, pl.ds(pl.multiple_of(off, 16), half), :]
                    tap = (2 - a) * 3 + 2 - b if back else a * 3 + b
                    d = dot(x, wt[tap * C:(tap + 1) * C, :], 1, 1 if back else 0)
                    acc = d if acc is None else acc + d
            out[pl.ds(pl.multiple_of(i * half, 16), half), :] = acc
            return c

        lax.fori_loop(0, 2, step, 0)

    def weight_grad(k, win, gs):
        for a in range(3):
            g = gs[2, (2 - a) * W:(2 - a) * W + MP, :]
            for b in range(3):
                t = a * 3 + b
                v = dot(win[b], g, 0, 0)
                wf[k, t * C:(t + 1) * C, :] = v
                wb[k, t * C:(t + 1) * C, :] = v.astype(BF16)

    pad_in[...] = jnp.zeros(pad_in.shape, F32)
    pad_in[1:T + 1, 1:T + 1, :] = feat[...].astype(F32)
    flat_in = pad_in[1:T + 1, 1:W + 1, :].reshape(M, C)
    rims = dot(own_rims, flat_in.astype(BF16)).astype(BF16)
    pl.semaphore_wait(barrier, S + F - 2)
    ex_start(0, send_mat, rims)

    cotp[...] = jnp.zeros(cotp.shape, F32)
    cotp[:, 0:H, :] = cot[...].astype(F32)
    r_up, c_up = iota((M, H * 16), 0), iota((M, H * 16), 1)
    spread = hot((r_up // (2 * W)) * 16 + (r_up % W) // 2 == c_up)
    up = dot(spread, cotp[...].reshape(H * 16, C).astype(BF16)) * 0.25
    gpad2[...] = jnp.zeros(gpad2.shape, F32)
    gpad2[2:T + 2, 2:T + 2, :] = up.reshape(T, W, C)[:, 0:T, :]
    windows(gpad2, gs2, T + 4)
    conv(gs2, w2, pg, MP, True)
    rims = dot(pad_rims, pg[...].astype(BF16)).astype(BF16)
    ex_start(2, recv_mat, rims)
    gact[...] = pg[...].reshape(T + 2, W, C)[1:T + 1]
    pad_act[...] = jnp.zeros(pad_act.shape, F32)
    gpad1[...] = jnp.zeros(gpad1.shape, F32)

    add_halo(pad_in, ex_wait(0, recv_mat))
    windows(pad_in, win_in, T + 2)
    conv(win_in, w1, hidden, M, False)
    hid = hidden[...] + b1[...]
    sig = 1.0 / (1.0 + jnp.exp(-hid))
    act = (hid * sig).astype(BF16)
    rims = dot(own_rims, act).astype(BF16)
    ex_start(1, send_mat, rims)
    pad_act[1:T + 1, 1:T + 1, :] = act.astype(F32).reshape(T, W, C)[:, 0:T, :]

    def fold(middle, arrived):
        hi, lo = split(arrived)
        back = dot(own_place, hi) + dot(own_place, lo)
        return middle[:, 1:T + 1, :] + back.reshape(T, W, C)[:, 0:T, :]

    ga = fold(gact, ex_wait(2, send_mat)).astype(BF16).astype(F32)
    slope = (sig * (1.0 + hid * (1.0 - sig))).reshape(T, W, C)[:, 0:T, :]
    gh = (ga * slope).astype(BF16).astype(F32)
    gpad1[2:T + 2, 2:T + 2, :] = gh
    windows(gpad1, gs1, T + 4)
    conv(gs1, w1, pg, MP, True)
    rims = dot(pad_rims, pg[...].astype(BF16)).astype(BF16)
    ex_start(3, recv_mat, rims)

    rows = wf.shape[1]

    def face_copy(k, st, f, f_in):
        return pltpu.make_async_remote_copy(
            src_ref=wb.at[k, pl.ds(pl.multiple_of(f * part, 16), part), :],
            dst_ref=w1in.at[k, f_in],
            send_sem=w_ss.at[k, 0, f], recv_sem=w_rs.at[k, 0, f_in],
            device_id=(f, sub), device_id_type=MESH)

    def sub_copy(k, j, j_in):
        return pltpu.make_async_remote_copy(
            src_ref=red.at[k, pl.ds(pl.multiple_of(j * chunk, 16), chunk), :],
            dst_ref=w2in.at[k, j_in],
            send_sem=w_ss.at[k, 1, j], recv_sem=w_rs.at[k, 1, j_in],
            device_id=(face, j), device_id_type=MESH)

    def sub_gather(k, j, own):
        place = gath.at[k, pl.ds(pl.multiple_of(face * part + own * chunk, 16), chunk), :]
        return pltpu.make_async_remote_copy(
            src_ref=place, dst_ref=place,
            send_sem=w_ss.at[k, 2, j], recv_sem=w_rs.at[k, 2, own],
            device_id=(face, j), device_id_type=MESH)

    def face_gather(k, f, own):
        place = gath.at[k, pl.ds(pl.multiple_of(own * part, 16), part), :]
        return pltpu.make_async_remote_copy(
            src_ref=place, dst_ref=place,
            send_sem=w_ss.at[k, 3, f], recv_sem=w_rs.at[k, 3, own],
            device_id=(f, sub), device_id_type=MESH)

    def reduce_start(k):
        peers(F, face, lambda f: face_copy(k, 0, f, face).start())

    def reduce_sub(k):
        peers(F, face, lambda f: face_copy(k, 0, f, f).wait_recv())
        accf[k] = wf[k, pl.ds(pl.multiple_of(face * part, 16), part), :]

        def add(f):
            accf[k] = accf[k] + w1in[k, f].astype(F32)
        peers(F, face, add)
        red[k] = accf[k].astype(BF16)
        peers(S, sub, lambda j: sub_copy(k, j, sub).start())

    def reduce_end(k):
        peers(S, sub, lambda j: sub_copy(k, j, j).wait_recv())
        own = pl.ds(pl.multiple_of(sub * chunk, 16), chunk)

        def step(d, tot):
            return tot + w2in[k, lax.rem(sub + d, S)].astype(F32)
        tot = lax.fori_loop(1, S, step, accf[k, own, :])
        gath[k, pl.ds(pl.multiple_of(face * part + sub * chunk, 16), chunk), :] = (tot * scale).astype(BF16)
        peers(S, sub, lambda j: sub_gather(k, j, sub).start())

    def gather_face(k):
        peers(S, sub, lambda j: sub_gather(k, j, j).wait_recv())
        peers(F, face, lambda f: face_gather(k, f, face).start())

    def gather_end(k, out):
        peers(F, face, lambda f: face_gather(k, f, f).wait_recv())
        out[...] = gath[k, 0:9 * C, :].astype(F32)

    def drain(k):
        peers(F, face, lambda f: face_copy(k, 0, f, face).wait_send())
        peers(S, sub, lambda j: sub_copy(k, j, sub).wait_send())
        peers(S, sub, lambda j: sub_gather(k, j, sub).wait_send())
        peers(F, face, lambda f: face_gather(k, f, face).wait_send())

    for k in range(2):
        wf[k, 9 * C:rows, :] = jnp.zeros((rows - 9 * C, C), F32)
        wb[k, 9 * C:rows, :] = jnp.zeros((rows - 9 * C, C), BF16)
    weight_grad(0, win_in, gs1)
    bias = jnp.sum(jnp.sum(gh, axis=0), axis=0, keepdims=True)
    bias = jnp.where(iota((16, C), 0) == 0, bias, 0.0)
    wf[0, 9 * C:9 * C + 16, :] = bias
    wb[0, 9 * C:9 * C + 16, :] = bias.astype(BF16)
    reduce_start(0)

    add_halo(pad_act, ex_wait(1, recv_mat))
    windows(pad_act, win_act, T + 2)
    weight_grad(1, win_act, gs2)
    reduce_start(1)
    reduce_sub(0)
    conv(win_act, w2, second, M, False)
    reduce_sub(1)
    hi, lo = split(second[...] + pad_in[1:T + 1, 1:W + 1, :].reshape(M, C))
    r_dn, c_dn = iota((H * 16, M), 0), iota((H * 16, M), 1)
    mean = hot((c_dn // (2 * W)) * 16 + (c_dn % W) // 2 == r_dn)
    down = (dot(mean, hi) + dot(mean, lo)) * 0.25
    pooled[...] = down.reshape(H, 16, C)[:, 0:H, :].astype(BF16)
    gact[...] = pg[...].reshape(T + 2, W, C)[1:T + 1]
    total = fold(gact, ex_wait(3, send_mat)) + gpad2[2:T + 2, 2:T + 2, :]
    gin[...] = total.astype(BF16)

    reduce_end(0)
    reduce_end(1)
    gather_face(0)
    gather_face(1)
    gather_end(0, gw1)
    gb1[...] = gath[0, 9 * C:9 * C + 16, :].astype(F32)[0:8]
    gather_end(1, gw2)
    for ph in range(4):
        ex_drain(ph)
    for k in range(2):
        drain(k)


def local(S, F, features, w_first, b_first, w_second, neighbours, rotations, cotangent):
    T, C = features.shape[1], features.shape[2]
    H = T // 2
    D = neighbours.shape[0]
    chunk = -(-(9 * C + 16) // (16 * D)) * 16
    rows, part = chunk * D, chunk * S
    K = (S + 4 * F) * W
    scale = 1.0 / math.sqrt(D * T * T)
    vm = pl.BlockSpec(memory_space=pltpu.VMEM)
    sm = pl.BlockSpec(memory_space=pltpu.SMEM)
    n = max(S, F)
    pooled, gin, gw1, gb1, gw2 = pl.pallas_call(
        functools.partial(kernel, S, F, chunk, scale),
        out_shape=(
            jax.ShapeDtypeStruct((H, H, C), BF16),
            jax.ShapeDtypeStruct((T, T, C), BF16),
            jax.ShapeDtypeStruct((9 * C, C), F32),
            jax.ShapeDtypeStruct((8, C), F32),
            jax.ShapeDtypeStruct((9 * C, C), F32),
        ),
        in_specs=[sm, sm, vm, vm, vm, vm, vm],
        out_specs=(vm,) * 5,
        scratch_shapes=[
            pltpu.VMEM((K, 4 * W), BF16),
            pltpu.VMEM((K, 4 * W), BF16),
            pltpu.VMEM((T + 2, W + 8, C), F32),
            pltpu.VMEM((T + 2, W + 8, C), F32),
            pltpu.VMEM((T + 4, W + 8, C), F32),
            pltpu.VMEM((T + 4, W + 8, C), F32),
            pltpu.VMEM((H, 16, C), F32),
            pltpu.VMEM((3, (T + 2) * W, C), BF16),
            pltpu.VMEM((3, (T + 2) * W, C), BF16),
            pltpu.VMEM((3, (T + 4) * W, C), BF16),
            pltpu.VMEM((3, (T + 4) * W, C), BF16),
            pltpu.VMEM((T * W, C), F32),
            pltpu.VMEM((T * W, C), F32),
            pltpu.VMEM(((T + 2) * W, C), F32),
            pltpu.VMEM((T, W, C), F32),
            pltpu.VMEM((4, K, C), BF16),
            pltpu.VMEM((4, K, C), BF16),
            pltpu.VMEM((2, rows, C), F32),
            pltpu.VMEM((2, rows, C), BF16),
            pltpu.VMEM((2, F, part, C), BF16),
            pltpu.VMEM((2, part, C), BF16),
            pltpu.VMEM((2, part, C), F32),
            pltpu.VMEM((2, S, chunk, C), BF16),
            pltpu.VMEM((2, rows, C), BF16),
            pltpu.SemaphoreType.DMA((4, S + F)),
            pltpu.SemaphoreType.DMA((4, S + F)),
            pltpu.SemaphoreType.DMA((2, 4, n)),
            pltpu.SemaphoreType.DMA((2, 4, n)),
        ],
        compiler_params=pltpu.CompilerParams(
            collective_id=0, has_side_effects=True, vmem_limit_bytes=56 * 1024 * 1024
        ),
        name="level",
    )(
        neighbours.reshape(-1), rotations.reshape(-1), features, cotangent,
        w_first.reshape(9 * C, C), b_first.reshape(1, C), w_second.reshape(9 * C, C),
    )
    return (pooled, gin, gw1.reshape(3, 3, C, C), gb1[0], gw2.reshape(3, 3, C, C))


def solution(mesh):
    tiles = P(("face", "sub"), None, None)
    return jax.shard_map(
        functools.partial(local, mesh.shape["sub"], mesh.shape["face"]),
        mesh=mesh,
        in_specs=(tiles, P(), P(), P(), P(), P(), tiles),
        out_specs=(tiles, tiles, P(), P(), P()),
        check_vma=False,
    )
```

```python
import functools
import math

import jax
import jax.numpy as jnp
from jax import lax
from jax.experimental import pallas as pl
from jax.experimental.pallas import tpu as pltpu
from jax.sharding import PartitionSpec as P

LANES = 128
W = 32
F32, BF16 = jnp.float32, jnp.bfloat16
MESH = pl.DeviceIdType.MESH


def iota(shape, dim):
    return lax.broadcasted_iota(jnp.int32, shape, dim)


def hot(mask):
    return jnp.where(mask, 1.0, 0.0).astype(BF16)


def dot(a, b, ca=1, cb=0):
    return lax.dot_general(a, b, (((ca,), (cb,)), ((), ())), preferred_element_type=F32)


def split(x):
    hi = x.astype(BF16)
    return hi, (x - hi.astype(F32)).astype(BF16)


def rim_pos(q, extent, pad):
    e, p = q >> 5, (q & (W - 1)) + pad
    far = extent - 1 + 2 * pad
    pos = jnp.where(e == 0, p, jnp.where(e == 1, p * W + far, jnp.where(e == 2, far * W + p, p * W)))
    return jnp.where((q & (W - 1)) < extent, pos, -1)


def pool_pos(r):
    return ((r >> 6) << 4) + ((r & (W - 1)) >> 1)


def kernel(S, F, chunk, scale, nbr, rot, feat, cot, w1, b1, w2,
           pooled, gin, gath,
           send_mat, recv_mat, pad_in, pad_act, gpad1, gpad2, cotp,
           win_in, win_act, gs1, gs2, hidden, second, pg, gact,
           ex_out, ex_in, wf, wb, w1in, red, accf, w2in, red2, acc2, w3in,
           ex_ss, ex_rs, w_ss, w_rs):
    T, C = feat.shape[0], feat.shape[2]
    H = T // 2
    face, sub = lax.axis_index("face"), lax.axis_index("sub")
    me = face * S + sub
    part = chunk * S
    A = 4 if S % 4 == 0 else 1
    B = S // A
    a_id, b_id = sub // B, lax.rem(sub, B)
    group = chunk * A
    M, MP = T * W, (T + 2) * W

    def peers(count, mine, body):
        def step(d, c):
            body(lax.rem(mine + d, count))
            return c
        lax.fori_loop(1, count, step, 0)

    barrier = pltpu.get_barrier_semaphore()
    peers(S, sub, lambda j: pl.semaphore_signal(barrier, inc=1, device_id=(face, j), device_id_type=MESH))
    peers(F, face, lambda f: pl.semaphore_signal(barrier, inc=1, device_id=(f, sub), device_id_type=MESH))

    p32 = iota((W, 4 * W), 0)
    c32 = iota((W, 4 * W), 1)

    def put_slot(k, hit, src, flip, edge):
        tgt = jnp.where(flip == 1, src * W + T - 1 - p32, src * W + p32)
        base = pl.multiple_of(k * W, W)
        send_mat[pl.ds(base, W), :] = hot((c32 == tgt) & (p32 < T) & (hit == 1))
        recv_mat[pl.ds(base, W), :] = hot((c32 == edge * W + p32) & (p32 < T) & (edge >= 0))

    def edge_code(tile, e):
        r = rot[tile * 4 + e]
        x = (e + 2) % 4
        src = (x + r) & 3
        odd = x % 2
        flip = jnp.where(r == 2, 1, jnp.where(r == 1, odd, jnp.where(r == 3, 1 - odd, 0)))
        return nbr[tile * 4 + e] == me, src, flip

    def in_face(j, c):
        hit, src, flip, edge = jnp.int32(0), jnp.int32(0), jnp.int32(0), jnp.int32(-1)
        for e in range(4):
            h, s, f = edge_code(face * S + j, e)
            hit = jnp.where(h, 1, hit)
            src = jnp.where(h, s, src)
            flip = jnp.where(h, f, flip)
            edge = jnp.where(nbr[me * 4 + e] == face * S + j, e, edge)
        put_slot(j, hit, src, flip, edge)
        return c

    lax.fori_loop(0, S, in_face, 0)

    def cross(f, c):
        for e in range(4):
            h, s, fl = edge_code(f * S + sub, e)
            other = f != face
            hit = jnp.where(h & other, 1, 0)
            edge = jnp.where((nbr[me * 4 + e] == f * S + sub) & other, e, -1)
            put_slot(S + f * 4 + e, hit, s, fl, edge)
        return c

    lax.fori_loop(0, F, cross, 0)

    for ph in range(4):
        ex_in[ph, pl.ds(pl.multiple_of(sub * W, W), W), :] = jnp.zeros((W, C), BF16)
        ex_in[ph, pl.ds(pl.multiple_of((S + 4 * face) * W, W), 4 * W), :] = jnp.zeros((4 * W, C), BF16)

    def ex_sub(ph, j, s_in, r_idx):
        return pltpu.make_async_remote_copy(
            src_ref=ex_out.at[ph, pl.ds(pl.multiple_of(j * W, W), W), :],
            dst_ref=ex_in.at[ph, pl.ds(pl.multiple_of(s_in * W, W), W), :],
            send_sem=ex_ss.at[ph, j], recv_sem=ex_rs.at[ph, r_idx],
            device_id=(face, j), device_id_type=MESH)

    def ex_face(ph, f, f_in):
        return pltpu.make_async_remote_copy(
            src_ref=ex_out.at[ph, pl.ds(pl.multiple_of((S + 4 * f) * W, W), 4 * W), :],
            dst_ref=ex_in.at[ph, pl.ds(pl.multiple_of((S + 4 * f_in) * W, W), 4 * W), :],
            send_sem=ex_ss.at[ph, S + f], recv_sem=ex_rs.at[ph, S + f_in],
            device_id=(f, sub), device_id_type=MESH)

    def ex_start(ph, mat, rims):
        ex_out[ph] = dot(mat[...], rims).astype(BF16)
        peers(S, sub, lambda j: ex_sub(ph, j, sub, sub).start())
        peers(F, face, lambda f: ex_face(ph, f, face).start())

    def ex_wait(ph, mat):
        peers(S, sub, lambda j: ex_sub(ph, j, j, j).wait_recv())
        peers(F, face, lambda f: ex_face(ph, f, f).wait_recv())
        return dot(mat[...], ex_in[ph], 0, 0)

    def ex_drain(ph):
        peers(S, sub, lambda j: ex_sub(ph, j, sub, sub).wait_send())
        peers(F, face, lambda f: ex_face(ph, f, face).wait_send())

    own_rims = hot(iota((4 * W, M), 1) == rim_pos(iota((4 * W, 1), 0), T, 0))
    pad_rims = hot(iota((4 * W, MP), 1) == rim_pos(iota((4 * W, 1), 0), T, 1))
    own_place = hot(iota((M, 4 * W), 0) == rim_pos(iota((1, 4 * W), 1), T, 0))
    pad_place = hot(iota((MP, 4 * W), 0) == rim_pos(iota((1, 4 * W), 1), T, 1))

    def windows(src, dst, rows):
        for b in range(3):
            dst[b] = src[:, b:b + W, :].reshape(rows * W, C).astype(BF16)

    def add_halo(padded, halo):
        placed = dot(pad_place, halo.astype(BF16)).reshape(T + 2, W, C)
        padded[:, 0:W, :] = padded[:, 0:W, :] + placed

    def conv(win, wt, out, rows, back):
        half = rows // 2

        def step(i, c):
            acc = None
            for a in range(3):
                for b in range(3):
                    off = pl.multiple_of(i * half, 16) + a * W
                    x = win[b, pl.ds(pl.multiple_of(off, 16), half), :]
                    tap = (2 - a) * 3 + 2 - b if back else a * 3 + b
                    d = dot(x, wt[tap * C:(tap + 1) * C, :], 1, 1 if back else 0)
                    acc = d if acc is None else acc + d
            out[pl.ds(pl.multiple_of(i * half, 16), half), :] = acc
            return c

        lax.fori_loop(0, 2, step, 0)

    def put(k, r, v):
        wf[k, r:r + v.shape[0], :] = v
        wb[k, r:r + v.shape[0], :] = v.astype(BF16)

    def weight_grad(k, win, gs):
        odd = None
        for t in range(9):
            a, b = t // 3, t % 3
            v = dot(win[b], gs[2, (2 - a) * W:(2 - a) * W + MP, :], 0, 0)
            put(k, t * C, v[:, 0:LANES])
            rest = v[:, LANES:C]
            if t % 2 == 0:
                odd = rest
            if t % 2 == 1 or t == 8:
                pair = jnp.concatenate([odd, rest], axis=1)
                put(k, (9 + t // 2) * C, pair)

    pad_in[...] = jnp.zeros(pad_in.shape, F32)
    pad_in[1:T + 1, 1:T + 1, :] = feat[...].astype(F32)
    flat_in = pad_in[1:T + 1, 1:W + 1, :].reshape(M, C)
    rims = dot(own_rims, flat_in.astype(BF16)).astype(BF16)
    pl.semaphore_wait(barrier, S + F - 2)
    ex_start(0, send_mat, rims)

    cotp[...] = jnp.zeros(cotp.shape, F32)
    cotp[:, 0:H, :] = cot[...].astype(F32)
    spread = hot(pool_pos(iota((M, 1), 0)) == iota((M, H * 16), 1))
    up = dot(spread, cotp[...].reshape(H * 16, C).astype(BF16)) * 0.25
    gpad2[...] = jnp.zeros(gpad2.shape, F32)
    gpad2[2:T + 2, 2:T + 2, :] = up.reshape(T, W, C)[:, 0:T, :]
    windows(gpad2, gs2, T + 4)
    conv(gs2, w2, pg, MP, True)
    rims = dot(pad_rims, pg[...].astype(BF16)).astype(BF16)
    ex_start(2, recv_mat, rims)
    gact[...] = pg[...].reshape(T + 2, W, C)[1:T + 1]
    pad_act[...] = jnp.zeros(pad_act.shape, F32)
    gpad1[...] = jnp.zeros(gpad1.shape, F32)

    add_halo(pad_in, ex_wait(0, recv_mat))
    windows(pad_in, win_in, T + 2)
    conv(win_in, w1, hidden, M, False)
    hid = hidden[...] + b1[...]
    sig = 1.0 / (1.0 + jnp.exp(-hid))
    act = (hid * sig).astype(BF16)
    rims = dot(own_rims, act).astype(BF16)
    ex_start(1, send_mat, rims)
    pad_act[1:T + 1, 1:T + 1, :] = act.astype(F32).reshape(T, W, C)[:, 0:T, :]

    def fold(middle, arrived):
        hi, lo = split(arrived)
        back = dot(own_place, hi) + dot(own_place, lo)
        return middle[:, 1:T + 1, :] + back.reshape(T, W, C)[:, 0:T, :]

    ga = fold(gact, ex_wait(2, send_mat)).astype(BF16).astype(F32)
    slope = (sig * (1.0 + hid * (1.0 - sig))).reshape(T, W, C)[:, 0:T, :]
    gh = (ga * slope).astype(BF16).astype(F32)
    gpad1[2:T + 2, 2:T + 2, :] = gh
    windows(gpad1, gs1, T + 4)
    conv(gs1, w1, pg, MP, True)
    rims = dot(pad_rims, pg[...].astype(BF16)).astype(BF16)
    ex_start(3, recv_mat, rims)

    rows = wf.shape[1]

    def face_copy(k, st, f, f_in):
        return pltpu.make_async_remote_copy(
            src_ref=wb.at[k, pl.ds(pl.multiple_of(f * part, 16), part), :],
            dst_ref=w1in.at[k, f_in],
            send_sem=w_ss.at[k, 0, f], recv_sem=w_rs.at[k, 0, f_in],
            device_id=(f, sub), device_id_type=MESH)

    def b_copy(k, j, j_in):
        return pltpu.make_async_remote_copy(
            src_ref=red.at[k, pl.ds(pl.multiple_of(j * group, 16), group), :],
            dst_ref=w2in.at[k, j_in],
            send_sem=w_ss.at[k, 1, j], recv_sem=w_rs.at[k, 1, j_in],
            device_id=(face, a_id * B + j), device_id_type=MESH)

    def a_copy(k, j, j_in):
        return pltpu.make_async_remote_copy(
            src_ref=red2.at[k, pl.ds(pl.multiple_of(j * chunk, 16), chunk), :],
            dst_ref=w3in.at[k, j_in],
            send_sem=w_ss.at[k, 2, j], recv_sem=w_rs.at[k, 2, j_in],
            device_id=(face, j * B + b_id), device_id_type=MESH)

    def spot(k, start, size):
        return gath.at[k, pl.ds(pl.multiple_of(start, 16), size), :]

    def a_gather(k, j, own):
        place = spot(k, face * part + b_id * group + own * chunk, chunk)
        return pltpu.make_async_remote_copy(
            src_ref=place, dst_ref=place,
            send_sem=w_ss.at[k, 3, j], recv_sem=w_rs.at[k, 3, own],
            device_id=(face, j * B + b_id), device_id_type=MESH)

    def b_gather(k, j, own):
        place = spot(k, face * part + own * group, group)
        return pltpu.make_async_remote_copy(
            src_ref=place, dst_ref=place,
            send_sem=w_ss.at[k, 4, j], recv_sem=w_rs.at[k, 4, own],
            device_id=(face, a_id * B + j), device_id_type=MESH)

    def face_gather(k, f, own):
        place = spot(k, own * part, part)
        return pltpu.make_async_remote_copy(
            src_ref=place, dst_ref=place,
            send_sem=w_ss.at[k, 5, f], recv_sem=w_rs.at[k, 5, own],
            device_id=(f, sub), device_id_type=MESH)

    def reduce_start(k):
        peers(F, face, lambda f: face_copy(k, 0, f, face).start())

    def summed(first, count, mine, ref, k):
        def step(d, tot):
            return tot + ref[k, lax.rem(mine + d, count)].astype(F32)
        return lax.fori_loop(1, count, step, first)

    def reduce_b(k):
        peers(F, face, lambda f: face_copy(k, 0, f, f).wait_recv())
        for r in range(B):
            at = pl.ds(pl.multiple_of(face * part + r * group, 16), group)
            tot = wf[k, at, :]
            for f in range(1, F):
                tot = tot + w1in[k, lax.rem(face + f, F), r * group:(r + 1) * group, :].astype(F32)
            accf[k, r * group:(r + 1) * group, :] = tot
            red[k, r * group:(r + 1) * group, :] = tot.astype(BF16)
        peers(B, b_id, lambda j: b_copy(k, j, b_id).start())

    def reduce_a(k):
        peers(B, b_id, lambda j: b_copy(k, j, j).wait_recv())
        tot = summed(accf[k, pl.ds(pl.multiple_of(b_id * group, 16), group), :], B, b_id, w2in, k)
        acc2[k] = tot
        red2[k] = tot.astype(BF16)
        peers(A, a_id, lambda j: a_copy(k, j, a_id).start())

    def gather_a(k):
        peers(A, a_id, lambda j: a_copy(k, j, j).wait_recv())
        tot = summed(acc2[k, pl.ds(pl.multiple_of(a_id * chunk, 16), chunk), :], A, a_id, w3in, k)
        own = pl.ds(pl.multiple_of(face * part + b_id * group + a_id * chunk, 16), chunk)
        gath[k, own, :] = (tot * scale).astype(BF16)
        peers(A, a_id, lambda j: a_gather(k, j, a_id).start())

    def gather_b(k):
        peers(A, a_id, lambda j: a_gather(k, j, j).wait_recv())
        peers(B, b_id, lambda j: b_gather(k, j, b_id).start())

    def gather_face(k):
        peers(B, b_id, lambda j: b_gather(k, j, j).wait_recv())
        peers(F, face, lambda f: face_gather(k, f, face).start())

    def gather_end(k):
        peers(F, face, lambda f: face_gather(k, f, f).wait_recv())

    def drain(k):
        peers(F, face, lambda f: face_copy(k, 0, f, face).wait_send())
        peers(B, b_id, lambda j: b_copy(k, j, b_id).wait_send())
        peers(A, a_id, lambda j: a_copy(k, j, a_id).wait_send())
        peers(A, a_id, lambda j: a_gather(k, j, a_id).wait_send())
        peers(B, b_id, lambda j: b_gather(k, j, b_id).wait_send())
        peers(F, face, lambda f: face_gather(k, f, face).wait_send())

    for k in range(2):
        put(k, 14 * C, jnp.zeros((rows - 14 * C, LANES), F32))
    weight_grad(0, win_in, gs1)
    bias = jnp.sum(jnp.sum(gh, axis=0), axis=0, keepdims=True)
    bias = jnp.concatenate([bias, jnp.zeros((1, 2 * LANES - C), F32)], axis=1)
    line = iota((16, LANES), 0)
    put(0, 14 * C, jnp.where(line == 0, bias[:, 0:LANES], jnp.where(line == 1, bias[:, LANES:], 0.0)))
    reduce_start(0)

    add_halo(pad_act, ex_wait(1, recv_mat))
    windows(pad_act, win_act, T + 2)
    reduce_b(0)
    weight_grad(1, win_act, gs2)
    reduce_start(1)
    reduce_a(0)
    conv(win_act, w2, second, M, False)
    reduce_b(1)
    gather_a(0)
    hi, lo = split(second[...] + pad_in[1:T + 1, 1:W + 1, :].reshape(M, C))
    mean = hot(pool_pos(iota((1, M), 1)) == iota((H * 16, M), 0))
    down = (dot(mean, hi) + dot(mean, lo)) * 0.25
    pooled[...] = down.reshape(H, 16, C)[:, 0:H, :].astype(BF16)
    gact[...] = pg[...].reshape(T + 2, W, C)[1:T + 1]
    total = fold(gact, ex_wait(3, send_mat)) + gpad2[2:T + 2, 2:T + 2, :]
    gin[...] = total.astype(BF16)

    gather_b(0)
    reduce_a(1)
    gather_a(1)
    gather_face(0)
    gather_b(1)
    gather_end(0)
    gather_face(1)
    gather_end(1)
    for ph in range(4):
        ex_drain(ph)
    for k in range(2):
        drain(k)


def finish(C, pooled_in, gin_in, gath, pooled, gin, gw1, gb1, gw2):
    pooled[...] = pooled_in[...]
    gin[...] = gin_in[...]
    for k, out in ((0, gw1), (1, gw2)):
        for t in range(9):
            left = gath[k, t * C:(t + 1) * C, :].astype(F32)
            pair = gath[k, (9 + t // 2) * C:(10 + t // 2) * C, :].astype(F32)
            half = C - LANES
            right = pair[:, 0:half] if t % 2 == 0 else pair[:, half:2 * half]
            out[t // 3, t % 3, :, 0:LANES] = left
            out[t // 3, t % 3, :, LANES:C] = right
    bias = gath[0, 14 * C:14 * C + 16, :].astype(F32)
    gb1[:, 0:LANES] = bias[0:1]
    gb1[:, LANES:C] = bias[1:2, 0:C - LANES]


def local(S, F, features, w_first, b_first, w_second, neighbours, rotations, cotangent):
    T, C = features.shape[1], features.shape[2]
    H = T // 2
    D = neighbours.shape[0]
    chunk = -(-(14 * C + 16) // (16 * D)) * 16
    A = 4 if S % 4 == 0 else 1
    B = S // A
    rows, part = chunk * D, chunk * S
    K = (S + 4 * F) * W
    scale = 1.0 / math.sqrt(D * T * T)
    vm = pl.BlockSpec(memory_space=pltpu.VMEM)
    sm = pl.BlockSpec(memory_space=pltpu.SMEM)
    n = max(S, F)
    pooled, gin, gath = pl.pallas_call(
        functools.partial(kernel, S, F, chunk, scale),
        out_shape=(
            jax.ShapeDtypeStruct((H, H, C), BF16),
            jax.ShapeDtypeStruct((T, T, C), BF16),
            jax.ShapeDtypeStruct((2, rows, LANES), BF16),
        ),
        in_specs=[sm, sm, vm, vm, vm, vm, vm],
        out_specs=(vm,) * 3,
        scratch_shapes=[
            pltpu.VMEM((K, 4 * W), BF16),
            pltpu.VMEM((K, 4 * W), BF16),
            pltpu.VMEM((T + 2, W + 8, C), F32),
            pltpu.VMEM((T + 2, W + 8, C), F32),
            pltpu.VMEM((T + 4, W + 8, C), F32),
            pltpu.VMEM((T + 4, W + 8, C), F32),
            pltpu.VMEM((H, 16, C), F32),
            pltpu.VMEM((3, (T + 2) * W, C), BF16),
            pltpu.VMEM((3, (T + 2) * W, C), BF16),
            pltpu.VMEM((3, (T + 4) * W, C), BF16),
            pltpu.VMEM((3, (T + 4) * W, C), BF16),
            pltpu.VMEM((T * W, C), F32),
            pltpu.VMEM((T * W, C), F32),
            pltpu.VMEM(((T + 2) * W, C), F32),
            pltpu.VMEM((T, W, C), F32),
            pltpu.VMEM((4, K, C), BF16),
            pltpu.VMEM((4, K, C), BF16),
            pltpu.VMEM((2, rows, LANES), F32),
            pltpu.VMEM((2, rows, LANES), BF16),
            pltpu.VMEM((2, F, part, LANES), BF16),
            pltpu.VMEM((2, part, LANES), BF16),
            pltpu.VMEM((2, part, LANES), F32),
            pltpu.VMEM((2, B, A * chunk, LANES), BF16),
            pltpu.VMEM((2, A * chunk, LANES), BF16),
            pltpu.VMEM((2, A * chunk, LANES), F32),
            pltpu.VMEM((2, A, chunk, LANES), BF16),
            pltpu.SemaphoreType.DMA((4, S + F)),
            pltpu.SemaphoreType.DMA((4, S + F)),
            pltpu.SemaphoreType.DMA((2, 6, n)),
            pltpu.SemaphoreType.DMA((2, 6, n)),
        ],
        compiler_params=pltpu.CompilerParams(
            collective_id=0, has_side_effects=True, vmem_limit_bytes=56 * 1024 * 1024
        ),
        name="level",
    )(
        neighbours.reshape(-1), rotations.reshape(-1), features, cotangent,
        w_first.reshape(9 * C, C), b_first.reshape(1, C), w_second.reshape(9 * C, C),
    )
    pooled, gin, gw1, gb1, gw2 = pl.pallas_call(
        functools.partial(finish, C),
        out_shape=(
            jax.ShapeDtypeStruct((H, H, C), BF16),
            jax.ShapeDtypeStruct((T, T, C), BF16),
            jax.ShapeDtypeStruct((3, 3, C, C), F32),
            jax.ShapeDtypeStruct((1, C), F32),
            jax.ShapeDtypeStruct((3, 3, C, C), F32),
        ),
        in_specs=[vm] * 3,
        out_specs=(vm,) * 5,
        compiler_params=pltpu.CompilerParams(vmem_limit_bytes=24 * 1024 * 1024),
        name="finish",
    )(pooled, gin, gath)
    return (pooled, gin, gw1, gb1.reshape(C), gw2)


def solution(mesh):
    tiles = P(("face", "sub"), None, None)
    return jax.shard_map(
        functools.partial(local, mesh.shape["sub"], mesh.shape["face"]),
        mesh=mesh,
        in_specs=(tiles, P(), P(), P(), P(), P(), tiles),
        out_specs=(tiles, tiles, P(), P(), P()),
        check_vma=False,
    )
```

```python
import functools
import math

import jax
import jax.numpy as jnp
from jax import lax
from jax.experimental import pallas as pl
from jax.experimental.pallas import tpu as pltpu
from jax.sharding import PartitionSpec as P

LANES = 128
W = 32
F32, BF16 = jnp.float32, jnp.bfloat16
MESH = pl.DeviceIdType.MESH


def iota(shape, dim):
    return lax.broadcasted_iota(jnp.int32, shape, dim)


def hot(mask):
    return jnp.where(mask, 1.0, 0.0).astype(BF16)


def dot(a, b, ca=1, cb=0):
    return lax.dot_general(a, b, (((ca,), (cb,)), ((), ())), preferred_element_type=F32)


def split(x):
    hi = x.astype(BF16)
    return hi, (x - hi.astype(F32)).astype(BF16)


def rim_pos(q, extent, pad):
    e, p = q >> 5, (q & (W - 1)) + pad
    far = extent - 1 + 2 * pad
    pos = jnp.where(e == 0, p, jnp.where(e == 1, p * W + far, jnp.where(e == 2, far * W + p, p * W)))
    return jnp.where((q & (W - 1)) < extent, pos, -1)


def pool_pos(r):
    return ((r >> 6) << 4) + ((r & (W - 1)) >> 1)


def kernel(S, F, chunk, scale, nbr, rot, feat, cot, w1, b1, w2,
           pooled, gin, gath,
           send_mat, recv_mat, pad_in, pad_act, gpad1, gpad2, cotp,
           win_in, win_act, gs1, gs2, hidden, second, pg, gact,
           ex_out, ex_in, wf, wb, w1in, red, accf, w2in, red2, acc2, w3in,
           ex_ss, ex_rs, w_ss, w_rs):
    T, C = feat.shape[0], feat.shape[2]
    H = T // 2
    face, sub = lax.axis_index("face"), lax.axis_index("sub")
    me = face * S + sub
    part = chunk * S
    A = 4 if S % 4 == 0 else 1
    B = S // A
    a_id, b_id = sub // B, lax.rem(sub, B)
    group = chunk * A
    M, MP = T * W, (T + 2) * W

    def peers(count, mine, body):
        def step(d, c):
            body(lax.rem(mine + d, count))
            return c
        lax.fori_loop(1, count, step, 0)

    barrier = pltpu.get_barrier_semaphore()
    peers(S, sub, lambda j: pl.semaphore_signal(barrier, inc=1, device_id=(face, j), device_id_type=MESH))
    peers(F, face, lambda f: pl.semaphore_signal(barrier, inc=1, device_id=(f, sub), device_id_type=MESH))

    p32 = iota((W, 4 * W), 0)
    c32 = iota((W, 4 * W), 1)

    def put_slot(k, hit, src, flip, edge):
        tgt = jnp.where(flip == 1, src * W + T - 1 - p32, src * W + p32)
        base = pl.multiple_of(k * W, W)
        send_mat[pl.ds(base, W), :] = hot((c32 == tgt) & (p32 < T) & (hit == 1))
        recv_mat[pl.ds(base, W), :] = hot((c32 == edge * W + p32) & (p32 < T) & (edge >= 0))

    def edge_code(tile, e):
        r = rot[tile, e]
        x = (e + 2) % 4
        src = (x + r) & 3
        odd = x % 2
        flip = jnp.where(r == 2, 1, jnp.where(r == 1, odd, jnp.where(r == 3, 1 - odd, 0)))
        return nbr[tile, e] == me, src, flip

    def in_face(j, c):
        hit, src, flip, edge = jnp.int32(0), jnp.int32(0), jnp.int32(0), jnp.int32(-1)
        for e in range(4):
            h, s, f = edge_code(face * S + j, e)
            hit = jnp.where(h, 1, hit)
            src = jnp.where(h, s, src)
            flip = jnp.where(h, f, flip)
            edge = jnp.where(nbr[me, e] == face * S + j, e, edge)
        put_slot(j, hit, src, flip, edge)
        return c

    lax.fori_loop(0, S, in_face, 0)

    def cross(f, c):
        for e in range(4):
            h, s, fl = edge_code(f * S + sub, e)
            other = f != face
            hit = jnp.where(h & other, 1, 0)
            edge = jnp.where((nbr[me, e] == f * S + sub) & other, e, -1)
            put_slot(S + f * 4 + e, hit, s, fl, edge)
        return c

    lax.fori_loop(0, F, cross, 0)

    for ph in range(4):
        ex_in[ph, pl.ds(pl.multiple_of(sub * W, W), W), :] = jnp.zeros((W, C), BF16)
        ex_in[ph, pl.ds(pl.multiple_of((S + 4 * face) * W, W), 4 * W), :] = jnp.zeros((4 * W, C), BF16)

    def ex_sub(ph, j, s_in, r_idx):
        return pltpu.make_async_remote_copy(
            src_ref=ex_out.at[ph, pl.ds(pl.multiple_of(j * W, W), W), :],
            dst_ref=ex_in.at[ph, pl.ds(pl.multiple_of(s_in * W, W), W), :],
            send_sem=ex_ss.at[ph, j], recv_sem=ex_rs.at[ph, r_idx],
            device_id=(face, j), device_id_type=MESH)

    def ex_face(ph, f, f_in):
        return pltpu.make_async_remote_copy(
            src_ref=ex_out.at[ph, pl.ds(pl.multiple_of((S + 4 * f) * W, W), 4 * W), :],
            dst_ref=ex_in.at[ph, pl.ds(pl.multiple_of((S + 4 * f_in) * W, W), 4 * W), :],
            send_sem=ex_ss.at[ph, S + f], recv_sem=ex_rs.at[ph, S + f_in],
            device_id=(f, sub), device_id_type=MESH)

    def ex_start(ph, mat, rims):
        ex_out[ph] = dot(mat[...], rims).astype(BF16)
        peers(S, sub, lambda j: ex_sub(ph, j, sub, sub).start())
        peers(F, face, lambda f: ex_face(ph, f, face).start())

    def ex_wait(ph, mat):
        peers(S, sub, lambda j: ex_sub(ph, j, j, j).wait_recv())
        peers(F, face, lambda f: ex_face(ph, f, f).wait_recv())
        return dot(mat[...], ex_in[ph], 0, 0)

    def ex_drain(ph):
        peers(S, sub, lambda j: ex_sub(ph, j, sub, sub).wait_send())
        peers(F, face, lambda f: ex_face(ph, f, face).wait_send())

    own_rims = hot(iota((4 * W, M), 1) == rim_pos(iota((4 * W, 1), 0), T, 0))
    pad_rims = hot(iota((4 * W, MP), 1) == rim_pos(iota((4 * W, 1), 0), T, 1))
    own_place = hot(iota((M, 4 * W), 0) == rim_pos(iota((1, 4 * W), 1), T, 0))
    pad_place = hot(iota((MP, 4 * W), 0) == rim_pos(iota((1, 4 * W), 1), T, 1))

    def windows(src, dst, rows):
        for b in range(3):
            dst[b] = src[:, b:b + W, :].reshape(rows * W, C).astype(BF16)

    def add_halo(padded, halo):
        placed = dot(pad_place, halo.astype(BF16)).reshape(T + 2, W, C)
        padded[:, 0:W, :] = padded[:, 0:W, :] + placed

    def conv(win, wt, out, rows, back):
        half = rows

        def step(i, c):
            acc = None
            for a in range(3):
                for b in range(3):
                    off = pl.multiple_of(i * half, 16) + a * W
                    x = win[b, pl.ds(pl.multiple_of(off, 16), half), :]
                    tap = (2 - a) * 3 + 2 - b if back else a * 3 + b
                    d = dot(x, wt[tap * C:(tap + 1) * C, :], 1, 1 if back else 0)
                    acc = d if acc is None else acc + d
            out[pl.ds(pl.multiple_of(i * half, 16), half), :] = acc
            return c

        lax.fori_loop(0, 1, step, 0)

    def put(k, r, v):
        wf[k, r:r + v.shape[0], :] = v
        wb[k, r:r + v.shape[0], :] = v.astype(BF16)

    def weight_grad(k, win, gs):
        odd = None
        for t in range(9):
            a, b = t // 3, t % 3
            v = dot(win[b], gs[2, (2 - a) * W:(2 - a) * W + MP, :], 0, 0)
            put(k, t * C, v[:, 0:LANES])
            rest = v[:, LANES:C]
            if t % 2 == 0:
                odd = rest
            if t % 2 == 1 or t == 8:
                pair = jnp.concatenate([odd, rest], axis=1)
                put(k, (9 + t // 2) * C, pair)

    pad_in[...] = jnp.zeros(pad_in.shape, F32)
    pad_in[1:T + 1, 1:T + 1, :] = feat[...].astype(F32)
    flat_in = pad_in[1:T + 1, 1:W + 1, :].reshape(M, C)
    rims = dot(own_rims, flat_in.astype(BF16)).astype(BF16)
    pl.semaphore_wait(barrier, S + F - 2)
    ex_start(0, send_mat, rims)

    cotp[...] = jnp.zeros(cotp.shape, F32)
    cotp[:, 0:H, :] = cot[...].astype(F32)
    spread = hot(pool_pos(iota((M, 1), 0)) == iota((M, H * 16), 1))
    up = dot(spread, cotp[...].reshape(H * 16, C).astype(BF16)) * 0.25
    gpad2[...] = jnp.zeros(gpad2.shape, F32)
    gpad2[2:T + 2, 2:T + 2, :] = up.reshape(T, W, C)[:, 0:T, :]
    windows(gpad2, gs2, T + 4)
    conv(gs2, w2, pg, MP, True)
    rims = dot(pad_rims, pg[...].astype(BF16)).astype(BF16)
    ex_start(2, recv_mat, rims)
    gact[...] = pg[...].reshape(T + 2, W, C)[1:T + 1]
    pad_act[...] = jnp.zeros(pad_act.shape, F32)
    gpad1[...] = jnp.zeros(gpad1.shape, F32)

    add_halo(pad_in, ex_wait(0, recv_mat))
    windows(pad_in, win_in, T + 2)
    conv(win_in, w1, hidden, M, False)
    hid = hidden[...] + b1[...]
    sig = 1.0 / (1.0 + jnp.exp(-hid))
    act = (hid * sig).astype(BF16)
    rims = dot(own_rims, act).astype(BF16)
    ex_start(1, send_mat, rims)
    pad_act[1:T + 1, 1:T + 1, :] = act.astype(F32).reshape(T, W, C)[:, 0:T, :]

    def fold(middle, arrived):
        hi, lo = split(arrived)
        back = dot(own_place, hi) + dot(own_place, lo)
        return middle[:, 1:T + 1, :] + back.reshape(T, W, C)[:, 0:T, :]

    ga = fold(gact, ex_wait(2, send_mat)).astype(BF16).astype(F32)
    slope = (sig * (1.0 + hid * (1.0 - sig))).reshape(T, W, C)[:, 0:T, :]
    gh = (ga * slope).astype(BF16).astype(F32)
    gpad1[2:T + 2, 2:T + 2, :] = gh
    windows(gpad1, gs1, T + 4)

    rows = wf.shape[1]

    def face_copy(k, st, f, f_in):
        return pltpu.make_async_remote_copy(
            src_ref=wb.at[k, pl.ds(pl.multiple_of(f * part, 16), part), :],
            dst_ref=w1in.at[k, f_in],
            send_sem=w_ss.at[k, 0, f], recv_sem=w_rs.at[k, 0, f_in],
            device_id=(f, sub), device_id_type=MESH)

    def b_copy(k, j, j_in):
        return pltpu.make_async_remote_copy(
            src_ref=red.at[k, pl.ds(pl.multiple_of(j * group, 16), group), :],
            dst_ref=w2in.at[k, j_in],
            send_sem=w_ss.at[k, 1, j], recv_sem=w_rs.at[k, 1, j_in],
            device_id=(face, a_id * B + j), device_id_type=MESH)

    def a_copy(k, j, j_in):
        return pltpu.make_async_remote_copy(
            src_ref=red2.at[k, pl.ds(pl.multiple_of(j * chunk, 16), chunk), :],
            dst_ref=w3in.at[k, j_in],
            send_sem=w_ss.at[k, 2, j], recv_sem=w_rs.at[k, 2, j_in],
            device_id=(face, j * B + b_id), device_id_type=MESH)

    def spot(k, start, size):
        return gath.at[k, pl.ds(pl.multiple_of(start, 16), size), :]

    def a_gather(k, j, own):
        place = spot(k, face * part + b_id * group + own * chunk, chunk)
        return pltpu.make_async_remote_copy(
            src_ref=place, dst_ref=place,
            send_sem=w_ss.at[k, 3, j], recv_sem=w_rs.at[k, 3, own],
            device_id=(face, j * B + b_id), device_id_type=MESH)

    def b_gather(k, j, own):
        place = spot(k, face * part + own * group, group)
        return pltpu.make_async_remote_copy(
            src_ref=place, dst_ref=place,
            send_sem=w_ss.at[k, 4, j], recv_sem=w_rs.at[k, 4, own],
            device_id=(face, a_id * B + j), device_id_type=MESH)

    def face_gather(k, f, own):
        place = spot(k, own * part, part)
        return pltpu.make_async_remote_copy(
            src_ref=place, dst_ref=place,
            send_sem=w_ss.at[k, 5, f], recv_sem=w_rs.at[k, 5, own],
            device_id=(f, sub), device_id_type=MESH)

    def reduce_start(k):
        peers(F, face, lambda f: face_copy(k, 0, f, face).start())

    def summed(first, count, mine, ref, k):
        def step(d, tot):
            return tot + ref[k, lax.rem(mine + d, count)].astype(F32)
        return lax.fori_loop(1, count, step, first)

    def reduce_b(k):
        peers(F, face, lambda f: face_copy(k, 0, f, f).wait_recv())
        for r in range(B):
            at = pl.ds(pl.multiple_of(face * part + r * group, 16), group)
            tot = wf[k, at, :]
            for f in range(1, F):
                tot = tot + w1in[k, lax.rem(face + f, F), r * group:(r + 1) * group, :].astype(F32)
            accf[k, r * group:(r + 1) * group, :] = tot
            red[k, r * group:(r + 1) * group, :] = tot.astype(BF16)
        peers(B, b_id, lambda j: b_copy(k, j, b_id).start())

    def reduce_a(k):
        peers(B, b_id, lambda j: b_copy(k, j, j).wait_recv())
        tot = summed(accf[k, pl.ds(pl.multiple_of(b_id * group, 16), group), :], B, b_id, w2in, k)
        acc2[k] = tot
        red2[k] = tot.astype(BF16)
        peers(A, a_id, lambda j: a_copy(k, j, a_id).start())

    def gather_a(k):
        peers(A, a_id, lambda j: a_copy(k, j, j).wait_recv())
        tot = summed(acc2[k, pl.ds(pl.multiple_of(a_id * chunk, 16), chunk), :], A, a_id, w3in, k)
        own = pl.ds(pl.multiple_of(face * part + b_id * group + a_id * chunk, 16), chunk)
        gath[k, own, :] = (tot * scale).astype(BF16)
        peers(A, a_id, lambda j: a_gather(k, j, a_id).start())

    def gather_b(k):
        peers(A, a_id, lambda j: a_gather(k, j, j).wait_recv())
        peers(B, b_id, lambda j: b_gather(k, j, b_id).start())

    def gather_face(k):
        peers(B, b_id, lambda j: b_gather(k, j, j).wait_recv())
        peers(F, face, lambda f: face_gather(k, f, face).start())

    def gather_end(k):
        peers(F, face, lambda f: face_gather(k, f, f).wait_recv())

    def drain(k):
        peers(F, face, lambda f: face_copy(k, 0, f, face).wait_send())
        peers(B, b_id, lambda j: b_copy(k, j, b_id).wait_send())
        peers(A, a_id, lambda j: a_copy(k, j, a_id).wait_send())
        peers(A, a_id, lambda j: a_gather(k, j, a_id).wait_send())
        peers(B, b_id, lambda j: b_gather(k, j, b_id).wait_send())
        peers(F, face, lambda f: face_gather(k, f, face).wait_send())

    for k in range(2):
        put(k, 14 * C, jnp.zeros((rows - 14 * C, LANES), F32))
    weight_grad(0, win_in, gs1)
    bias = jnp.sum(jnp.sum(gh, axis=0), axis=0, keepdims=True)
    bias = jnp.concatenate([bias, jnp.zeros((1, 2 * LANES - C), F32)], axis=1)
    line = iota((16, LANES), 0)
    put(0, 14 * C, jnp.where(line == 0, bias[:, 0:LANES], jnp.where(line == 1, bias[:, LANES:], 0.0)))
    reduce_start(0)

    add_halo(pad_act, ex_wait(1, recv_mat))
    windows(pad_act, win_act, T + 2)
    reduce_b(0)
    weight_grad(1, win_act, gs2)
    reduce_start(1)
    conv(gs1, w1, pg, MP, True)
    rims = dot(pad_rims, pg[...].astype(BF16)).astype(BF16)
    ex_start(3, recv_mat, rims)
    reduce_a(0)
    reduce_b(1)
    conv(win_act, w2, second, M, False)
    gather_a(0)
    hi, lo = split(second[...] + pad_in[1:T + 1, 1:W + 1, :].reshape(M, C))
    mean = hot(pool_pos(iota((1, M), 1)) == iota((H * 16, M), 0))
    down = (dot(mean, hi) + dot(mean, lo)) * 0.25
    pooled[...] = down.reshape(H, 16, C)[:, 0:H, :].astype(BF16)
    reduce_a(1)
    gather_b(0)
    gact[...] = pg[...].reshape(T + 2, W, C)[1:T + 1]
    total = fold(gact, ex_wait(3, send_mat)) + gpad2[2:T + 2, 2:T + 2, :]
    gin[...] = total.astype(BF16)
    gather_a(1)
    gather_face(0)
    gather_b(1)
    gather_end(0)
    gather_face(1)
    gather_end(1)
    for ph in range(4):
        ex_drain(ph)
    for k in range(2):
        drain(k)


def finish(C, pooled_in, gin_in, gath, pooled, gin, gw1, gb1, gw2):
    pooled[...] = pooled_in[...]
    gin[...] = gin_in[...]
    for k, out in ((0, gw1), (1, gw2)):
        for t in range(9):
            left = gath[k, t * C:(t + 1) * C, :].astype(F32)
            pair = gath[k, (9 + t // 2) * C:(10 + t // 2) * C, :].astype(F32)
            half = C - LANES
            right = pair[:, 0:half] if t % 2 == 0 else pair[:, half:2 * half]
            out[t // 3, t % 3, :, 0:LANES] = left
            out[t // 3, t % 3, :, LANES:C] = right
    bias = gath[0, 14 * C:14 * C + 16, :].astype(F32)
    gb1[:, 0:LANES] = bias[0:1]
    gb1[:, LANES:C] = bias[1:2, 0:C - LANES]


def local(S, F, features, w_first, b_first, w_second, neighbours, rotations, cotangent):
    T, C = features.shape[1], features.shape[2]
    H = T // 2
    D = neighbours.shape[0]
    chunk = -(-(14 * C + 16) // (16 * D)) * 16
    A = 4 if S % 4 == 0 else 1
    B = S // A
    rows, part = chunk * D, chunk * S
    K = (S + 4 * F) * W
    scale = 1.0 / math.sqrt(D * T * T)
    vm = pl.BlockSpec(memory_space=pltpu.VMEM)
    sm = pl.BlockSpec(memory_space=pltpu.SMEM)
    n = max(S, F)
    pooled, gin, gath = pl.pallas_call(
        functools.partial(kernel, S, F, chunk, scale),
        out_shape=(
            jax.ShapeDtypeStruct((H, H, C), BF16),
            jax.ShapeDtypeStruct((T, T, C), BF16),
            jax.ShapeDtypeStruct((2, rows, LANES), BF16),
        ),
        in_specs=[sm, sm, vm, vm, vm, vm, vm],
        out_specs=(vm,) * 3,
        scratch_shapes=[
            pltpu.VMEM((K, 4 * W), BF16),
            pltpu.VMEM((K, 4 * W), BF16),
            pltpu.VMEM((T + 2, W + 8, C), F32),
            pltpu.VMEM((T + 2, W + 8, C), F32),
            pltpu.VMEM((T + 4, W + 8, C), F32),
            pltpu.VMEM((T + 4, W + 8, C), F32),
            pltpu.VMEM((H, 16, C), F32),
            pltpu.VMEM((3, (T + 2) * W, C), BF16),
            pltpu.VMEM((3, (T + 2) * W, C), BF16),
            pltpu.VMEM((3, (T + 4) * W, C), BF16),
            pltpu.VMEM((3, (T + 4) * W, C), BF16),
            pltpu.VMEM((T * W, C), F32),
            pltpu.VMEM((T * W, C), F32),
            pltpu.VMEM(((T + 2) * W, C), F32),
            pltpu.VMEM((T, W, C), F32),
            pltpu.VMEM((4, K, C), BF16),
            pltpu.VMEM((4, K, C), BF16),
            pltpu.VMEM((2, rows, LANES), F32),
            pltpu.VMEM((2, rows, LANES), BF16),
            pltpu.VMEM((2, F, part, LANES), BF16),
            pltpu.VMEM((2, part, LANES), BF16),
            pltpu.VMEM((2, part, LANES), F32),
            pltpu.VMEM((2, B, A * chunk, LANES), BF16),
            pltpu.VMEM((2, A * chunk, LANES), BF16),
            pltpu.VMEM((2, A * chunk, LANES), F32),
            pltpu.VMEM((2, A, chunk, LANES), BF16),
            pltpu.SemaphoreType.DMA((4, S + F)),
            pltpu.SemaphoreType.DMA((4, S + F)),
            pltpu.SemaphoreType.DMA((2, 6, n)),
            pltpu.SemaphoreType.DMA((2, 6, n)),
        ],
        compiler_params=pltpu.CompilerParams(
            collective_id=0, has_side_effects=True, vmem_limit_bytes=56 * 1024 * 1024
        ),
        name="level",
    )(
        neighbours, rotations, features, cotangent,
        w_first.reshape(9 * C, C), b_first.reshape(1, C), w_second.reshape(9 * C, C),
    )
    pooled, gin, gw1, gb1, gw2 = pl.pallas_call(
        functools.partial(finish, C),
        out_shape=(
            jax.ShapeDtypeStruct((H, H, C), BF16),
            jax.ShapeDtypeStruct((T, T, C), BF16),
            jax.ShapeDtypeStruct((3, 3, C, C), F32),
            jax.ShapeDtypeStruct((1, C), F32),
            jax.ShapeDtypeStruct((3, 3, C, C), F32),
        ),
        in_specs=[vm] * 3,
        out_specs=(vm,) * 5,
        compiler_params=pltpu.CompilerParams(vmem_limit_bytes=24 * 1024 * 1024),
        name="finish",
    )(pooled, gin, gath)
    return (pooled, gin, gw1, gb1.reshape(C), gw2)


def solution(mesh):
    tiles = P(("face", "sub"), None, None)
    return jax.shard_map(
        functools.partial(local, mesh.shape["sub"], mesh.shape["face"]),
        mesh=mesh,
        in_specs=(tiles, P(), P(), P(), P(), P(), tiles),
        out_specs=(tiles, tiles, P(), P(), P()),
        check_vma=False,
    )
```
